256 devices in a mesh: pole: 4 (over z_lo), prow: 8 (over x, core), pcol: 8 (over y, z_hi).
Axes of the slice: x: 4, y: 4, z: 8 (z_hi: 2, z_lo: 4; z = z_hi * 4 + z_lo), core: 2. Of those that a mesh axis runs over, the one named last changes fastest.
Arguments:
- lower: float32 [4, 4096, 4096], P('pole', 'prow', 'pcol'), may hold values from -0.1875 to 0.1875
- upper: float32 [4, 4096, 4096], P('pole', 'prow', 'pcol'), may hold values from -0.1875 to 0.1875
- dinv: float32 [4, 4096, 4096], P('pole', 'prow', 'pcol'), may hold values from -6 to 6
- pole_weight: float32 [4], P('pole'), may hold values from 0.25 to 1
- block_pattern: int32 [16, 16], replicated, may hold values 0 or 1
Outputs:
- density: float32 [4096, 4096], P('prow', 'pcol')
The draws below stay inside these ranges and needn't reach their ends.
All inputs are finite; a program needn't handle non-finite values.
Results may differ from the reference program's by a relative error of at most 0.0001.
Values sent between devices are 32-bit elements; how exact they have to be, the bound alone decides.
A program may use at most 64 MiB of HBM per device.

```python
import jax
import jax.numpy as jnp
import numpy as np
from jax import lax

B = 256
NSUP = 16
M = 4096
POLES = 4


def place_ends(result, rng, smallest, top_value):
    place = [jax.random.randint(jax.random.fold_in(rng, axis), (), 0, length) for axis, length in enumerate(result.shape)]
    main_axis = result.shape.index(max(result.shape))
    beside = place[:main_axis] + [(place[main_axis] + 1) % result.shape[main_axis]] + place[main_axis + 1:]
    return result.at[tuple(place)].set(smallest).at[tuple(beside)].set(top_value)


def block_levels(rng, shape, split, low, high):
    gain = 1.0
    for dim, shards_of in split:
        steps = jax.random.uniform(jax.random.fold_in(jax.random.fold_in(rng, 6), dim), (shards_of,), jnp.float32, low / len(split), high / len(split))
        gain = gain * jnp.repeat(jnp.exp(steps), shape[dim] // shards_of).reshape((-1,) + (1,) * (len(shape) - 1 - dim))
    return gain


def scatter_about(key, extent, width, bound, cuts=(), kind=jnp.bfloat16):
    factor_of = block_levels(key, extent, cuts, -0.22, 0.18) if cuts else 1.0
    drawn = jax.random.normal(key, extent, jnp.float32) * width * factor_of
    return jnp.minimum(jnp.maximum(drawn, -bound), bound).astype(kind)


def setup_inputs(seed: int = 0) -> dict:
    key_of = jax.random.split(jax.random.key(seed), 6)
    return {
        "lower": scatter_about(key_of[0], (POLES, M, M), (4 * B) ** -0.5, 0.1875, ((0, 4), (1, 8), (2, 8)), jnp.float32),
        "upper": scatter_about(key_of[1], (POLES, M, M), (4 * B) ** -0.5, 0.1875, ((0, 4), (1, 8), (2, 8)), jnp.float32),
        "dinv": scatter_about(key_of[2], (POLES, M, M), 1.0, 6.0, ((0, 4), (1, 8), (2, 8)), jnp.float32),
        "pole_weight": jnp.clip(0.25 + 0.75 * jax.random.uniform(key_of[3], (POLES,), jnp.float32) ** block_levels(key_of[3], (POLES,), ((0, 4),), -0.2, 0.2), 0.25, 1.0),
        "block_pattern": place_ends((jax.random.randint(key_of[4], (NSUP, NSUP), 0, 4) < 3).astype(jnp.int32), jax.random.fold_in(key_of[4], 1), 0, 1),
    }


def tier_of(supers):
    halves = supers // 2
    upper_tier = jnp.where(halves < 4, 1, 2)
    return jnp.where(supers % 2 == 0, 0, upper_tier)


def node_of(supers):
    halves = supers // 2
    upper_node = jnp.where(halves < 4, halves // 2, 0)
    return jnp.where(supers % 2 == 0, halves // 2, upper_node)


def above(elders, youngers):
    tier_old = tier_of(elders)[:, None]
    tier_new = tier_of(youngers)[None, :]
    node_old = node_of(elders)[:, None]
    node_new = node_of(youngers)[None, :]
    shift_by = jnp.maximum(tier_old - tier_new, 0)
    return (tier_old > tier_new) & (node_old == jnp.right_shift(node_new, shift_by))


def same_node(firsts, seconds):
    tier_same = tier_of(firsts)[:, None] == tier_of(seconds)[None, :]
    node_same = node_of(firsts)[:, None] == node_of(seconds)[None, :]
    return tier_same & node_same


def static_tier(number):
    if number % 2 == 0:
        return 0
    if number // 2 < 4:
        return 1
    return 2


def element_index(supers):
    return np.concatenate([np.arange(number * B, (number + 1) * B) for number in supers]).astype(np.int32)


def expand(mask):
    flags = mask.astype(jnp.float32)
    return jnp.repeat(jnp.repeat(flags, B, axis=0), B, axis=1)


def highest(left, right):
    return jnp.dot(left, right, precision=lax.Precision.HIGHEST, preferred_element_type=jnp.float32)


def pick(matrix, rows, cols):
    return matrix[rows[:, None], cols[None, :]]


def invert_pole(lower, upper, dinv, block_pattern):
    supers = jnp.arange(NSUP)
    elder = above(supers, supers)
    keep = elder & (block_pattern > 0)
    lmat = lower * expand(keep)
    umat = upper * expand(keep.T)
    elder_mask = expand(elder)
    share_mask = expand(same_node(supers, supers))
    top_flags = jnp.asarray(np.array([static_tier(number) == 2 for number in range(NSUP)]))
    greens = dinv * share_mask * expand(top_flags[:, None] & top_flags[None, :])
    higher = element_index([number for number in range(NSUP) if number % 2 == 1])
    for tier_now in (1, 0):
        columns = element_index([number for number in range(NSUP) if static_tier(number) == tier_now])
        known = pick(greens, higher, higher)
        panel = -highest(known, pick(lmat, higher, columns)) * pick(elder_mask, higher, columns)
        row_factor = pick(umat, columns, higher)
        rowpart = -highest(row_factor, known) * pick(elder_mask.T, columns, higher)
        share = pick(share_mask, columns, columns)
        diagpart = (pick(dinv, columns, columns) - highest(row_factor, panel)) * share
        greens = greens.at[higher[:, None], columns[None, :]].add(panel)
        greens = greens.at[columns[:, None], higher[None, :]].add(rowpart)
        greens = greens.at[columns[:, None], columns[None, :]].add(diagpart)
    return greens


def reference(lower, upper, dinv, pole_weight, block_pattern):
    density = jnp.zeros((M, M), jnp.float32)
    for pole_now in range(POLES):
        greens = invert_pole(lower[pole_now], upper[pole_now], dinv[pole_now], block_pattern)
        density = density + pole_weight[pole_now] * greens
    return density
```

```python
import jax
import jax.numpy as jnp
from jax import lax
from jax.experimental import pallas as pl
from jax.experimental.pallas import tpu as pltpu
from jax.sharding import PartitionSpec as P

B = 256
H = B // 2
MESH = pl.DeviceIdType.MESH
N_SEND = 128


def split(values):
    high = values.astype(jnp.bfloat16)
    low = (values - high.astype(jnp.float32)).astype(jnp.bfloat16)
    return high, low


def block_dot(left, right):
    lh, ll = split(left)
    rh, rl = split(right)
    big = jnp.concatenate([lh, lh, ll], axis=1)
    tall = jnp.concatenate([rh, rl, rh], axis=0)
    return jnp.dot(big, tall, preferred_element_type=jnp.float32)


def kernel(
    low_ref, up_ref, din_ref, weight_ref, pat_ref, out_ref,
    row_o, row_u, col_la, col_lt, col_l1, col_gt, col_ga, col_pt, col_pa,
    part, inbox,
    send_sem, ro_sem, ru_sem, la_sem, lt_sem, l1_sem, gt_sem, ga_sem, pt_sem, pa_sem, red_sem,
):
    p = lax.axis_index("pole")
    i = lax.axis_index("prow")
    j = lax.axis_index("pcol")
    x, c = i // 2, i % 2
    y, h = j // 2, j % 2
    sib = (p, 2 * x + 1 - c, j)
    partner = (p, i, 2 * y + 1 - h)
    jp = 2 * y + 1 - h

    def xdev(xx):
        return (p, 2 * xx + c, j)

    def ydev(yy):
        return (p, i, 2 * yy + h)

    barrier = pltpu.get_barrier_semaphore()
    others = [sib, partner]
    for d in (1, 2, 3):
        others += [xdev((x + d) % 4), ydev((y + d) % 4), ((p + d) % 4, i, j)]
    for dev in others:
        pl.semaphore_signal(barrier, inc=1, device_id=dev, device_id_type=MESH)

    yes = p >= 0
    sends = []

    def send(cond, src, dst, rsem, dev):
        copy = pltpu.make_async_remote_copy(
            src_ref=src, dst_ref=dst, send_sem=send_sem.at[len(sends)], recv_sem=rsem,
            device_id=dev, device_id_type=MESH,
        )
        sends.append((cond, copy))
        pl.when(cond)(lambda: copy.start())

    def arrive(cond, dst, rsem):
        copy = pltpu.make_async_remote_copy(
            src_ref=dst, dst_ref=dst, send_sem=send_sem.at[0], recv_sem=rsem,
            device_id=sib, device_id_type=MESH,
        )
        pl.when(cond)(lambda: copy.wait_recv())

    def flag(a, b):
        return jnp.where(pat_ref[a, b] > 0, 1.0, 0.0).astype(jnp.float32)

    weight = weight_ref[0]
    low_oo = flag(2 * i + 1, 2 * j + 1)
    low_oe = flag(2 * i + 1, 2 * j)
    up_oo = flag(2 * j + 1, 2 * i + 1)
    up_eo = flag(2 * j + 1, 2 * i)

    top_row = x >= 2
    top_col = y >= 2
    odd_live = top_row | top_col | (x == y)
    col_live = top_row | (x == y // 2)
    row_live = top_col | (y == x // 2)
    diag_live = x == y
    even, odd = pl.ds(0, B), pl.ds(B, B)
    minus_y = (2 * (y // 2), 2 * (y // 2) + 1)

    @pl.when(top_row & ~top_col)
    def _():
        block = low_ref[0, odd, odd] * low_oo
        row_o[j] = block
        col_l1[i - 4] = block

    @pl.when(top_row & top_col)
    def _():
        block = din_ref[0, odd, odd]
        row_o[j] = block
        col_gt[i - 4] = block

    @pl.when(~top_row & top_col)
    def _():
        row_o[j] = up_ref[0, odd, odd] * up_oo

    @pl.when(~top_row & (x == y))
    def _():
        row_o[j] = din_ref[0, odd, odd]

    @pl.when(x == y // 2)
    def _():
        col_la[c] = low_ref[0, odd, even] * low_oe

    @pl.when(row_live)
    def _():
        row_u[j] = up_ref[0, even, odd] * up_eo

    pl.semaphore_wait(barrier, 11)

    def needs_o(src, dst):
        wide = jnp.where(x == 1, dst >= 1, yes)
        return (((src >= 2) & wide) | ((src < 2) & (dst // 2 == src))) & (top_row | (src >= 2) | (src == x))

    def needs_u(src, dst):
        live = (src >= 2) | (src == x // 2)
        return live & ((dst >= 2) | (dst == x // 2) | (dst == x))

    def row_send(buf, sem, needs, slot):
        for d in (1, 3, 2):
            yy = (y + d) % 4
            send(needs(y, yy), buf.at[slot], buf.at[slot], sem.at[slot], ydev(yy))

    def row_arrive(buf, sem, needs, src):
        cond = needs(src, y) & (src != y)
        for half in (0, 1):
            slot = 2 * src + half
            arrive(cond, buf.at[slot], sem.at[slot])

    def col_send(buf, sem, base, live, needs):
        slot = i - base
        slot = jnp.where(live, slot, 0)
        for d in (1, 3, 2):
            xx = (x + d) % 4
            send(live & needs(xx), buf.at[slot], buf.at[slot], sem.at[slot], xdev(xx))
        send(live & needs(x), buf.at[slot], buf.at[slot], sem.at[slot], sib)

    def col_arrive(buf, sem, base, xs, live, needs):
        for xx in xs:
            near = 2 * xx + c - base
            far = 2 * xx + 1 - c - base
            cond = live(xx) & needs(x) & (xx != x)
            arrive(cond, buf.at[near], sem.at[near])
            send(cond, buf.at[near], buf.at[near], sem.at[near], sib)
        for xx in xs:
            far = 2 * xx + 1 - c - base
            arrive(live(xx) & needs(x), buf.at[far], sem.at[far])

    halves = ((0, p), (1, 3 - p))

    def toward(q, half):
        pole = q if half == 0 else 3 - q
        return (pole, i, j)

    def rows_of(quad, half):
        return pl.ds((quad // 2) * B + half * H, H), pl.ds((quad % 2) * B, B)

    def red_a(quad, live):
        for half, q in halves:
            src = part.at[quad, pl.ds(half * H, H)]
            send(live & (q == 0), src, inbox.at[quad, half, 0], red_sem.at[quad, half, 0], toward(1, half))
            send(live & (q == 3), src, inbox.at[quad, half, 1], red_sem.at[quad, half, 1], toward(2, half))

    def red_b(quad, live):
        for half, q in halves:
            arrive(live & (q == 2), inbox.at[quad, half, 1], red_sem.at[quad, half, 1])
            rows = pl.ds(half * H, H)

            @pl.when(live & (q == 2))
            def _():
                part[quad, rows] = part[quad, rows] + inbox[quad, half, 1]

            src = part.at[quad, rows]
            send(live & (q == 2), src, inbox.at[quad, half, 1], red_sem.at[quad, half, 1], toward(1, half))

    def red_c(quad, live):
        for half, q in halves:
            arrive(live & (q == 1), inbox.at[quad, half, 0], red_sem.at[quad, half, 0])
            arrive(live & (q == 1), inbox.at[quad, half, 1], red_sem.at[quad, half, 1])
            rows = pl.ds(half * H, H)
            orow, ocol = rows_of(quad, half)

            @pl.when(live & (q == 1))
            def _():
                out_ref[orow, ocol] = part[quad, rows] + inbox[quad, half, 0] + inbox[quad, half, 1]

            place = out_ref.at[orow, ocol]
            send(live & (q == 1), place, place, red_sem.at[quad, half, 2], toward(2, half))
            send(live & (q == 1), place, place, red_sem.at[quad, half, 2], toward(0, half))

    def red_d(quad, live):
        for half, q in halves:
            place = out_ref.at[rows_of(quad, half)]
            arrive(live & (q == 2), place, red_sem.at[quad, half, 2])
            send(live & (q == 2), place, place, red_sem.at[quad, half, 2], toward(3, half))

    def red_e(quad, live):
        for half, q in halves:
            place = out_ref.at[rows_of(quad, half)]
            arrive(live & ((q == 0) | (q == 3)), place, red_sem.at[quad, half, 2])

    def sum_dots(pairs):
        total = None
        for left, right in pairs:
            term = block_dot(left, right)
            total = term if total is None else total + term
        return total

    send(odd_live, row_o.at[j], row_o.at[j], ro_sem.at[j], partner)
    row_send(row_o, ro_sem, needs_o, j)
    la_live = x == y // 2
    la_needs = lambda xx: (xx >= 2) | (xx == y // 2)
    col_send(col_la, la_sem, 2 * (y // 2), la_live, la_needs)
    l1_live = top_row & ~top_col
    l1_needs = lambda xx: (xx >= 2) & (y < 2)
    col_send(col_l1, l1_sem, 4, l1_live, l1_needs)
    gt_needs = lambda xx: (y >= 2) | (xx // 2 == y) | ((xx == 1) & (y == 1))
    gt_any = lambda xx: xx >= 2
    col_send(col_gt, gt_sem, 4, top_row & top_col, gt_needs)

    @pl.when(~odd_live)
    def _():
        out_ref[odd, odd] = jnp.zeros((B, B), jnp.float32)

    @pl.when(~col_live)
    def _():
        out_ref[odd, even] = jnp.zeros((B, B), jnp.float32)

    @pl.when(~row_live)
    def _():
        out_ref[even, odd] = jnp.zeros((B, B), jnp.float32)

    @pl.when(~diag_live)
    def _():
        out_ref[even, even] = jnp.zeros((B, B), jnp.float32)

    arrive(odd_live, row_o.at[jp], ro_sem.at[jp])
    row_send(row_o, ro_sem, needs_o, jp)
    send(row_live, row_u.at[j], row_u.at[j], ru_sem.at[j], partner)
    row_send(row_u, ru_sem, needs_u, j)

    la_any = lambda xx: yes
    for shift in (0,):
        xx = y // 2
        near, far = c, 1 - c
        cond = la_needs(x) & (x != xx)
        arrive(cond, col_la.at[near], la_sem.at[near])
        send(cond, col_la.at[near], col_la.at[near], la_sem.at[near], sib)
        arrive(la_needs(x), col_la.at[far], la_sem.at[far])
    col_arrive(col_l1, l1_sem, 4, (2, 3), lambda xx: yes, l1_needs)
    for src in (0, 1):
        row_arrive(row_o, ro_sem, needs_o, src)

    @pl.when(top_row)
    def _():
        through = sum_dots([(row_o[minus_y[k]], col_la[k]) for k in (0, 1)])
        col_lt[i - 4] = low_ref[0, odd, even] * low_oe - through

    lt_needs = lambda xx: xx >= 2
    col_send(col_lt, lt_sem, 4, top_row, lt_needs)
    for src in (2, 3):
        row_arrive(row_o, ro_sem, needs_o, src)

    @pl.when(top_row & ~top_col)
    def _():
        col_gt[i - 4] = -sum_dots([(row_o[4 + k], col_l1[k]) for k in range(4)])

    col_send(col_gt, gt_sem, 4, top_row & ~top_col, gt_needs)

    @pl.when(top_row)
    def _():
        part[3] = col_gt[i - 4] * weight

    red_a(3, top_row)
    col_arrive(col_lt, lt_sem, 4, (2, 3), gt_any, lt_needs)

    @pl.when(top_row)
    def _():
        col_pt[i - 4] = -sum_dots([(row_o[4 + k], col_lt[k]) for k in range(4)])
        part[2] = col_pt[i - 4] * weight

    pt_needs = lambda xx: (xx == y // 2) | (xx == y)
    col_send(col_pt, pt_sem, 4, top_row, pt_needs)
    red_a(2, top_row)

    arrive(row_live, row_u.at[jp], ru_sem.at[jp])
    row_send(row_u, ru_sem, needs_u, jp)

    col_arrive(col_gt, gt_sem, 4, (2, 3), gt_any, gt_needs)
    ga_live = (x < 2) & (top_col | (x == y))

    @pl.when(ga_live)
    def _():
        base = jnp.where(x == y, 1.0, 0.0).astype(jnp.float32)
        folded = sum_dots([(row_o[4 + k], col_gt[k]) for k in range(4)])
        col_ga[c] = din_ref[0, odd, odd] * base - folded
        part[3] = col_ga[c] * weight

    for d in (1, 3, 2):
        xx = (x + d) % 4
        send(ga_live & (xx // 2 == x), col_ga.at[c], col_ga.at[2 + c], ga_sem.at[c], xdev(xx))
    send(ga_live & (x == 0), col_ga.at[c], col_ga.at[2 + c], ga_sem.at[c], sib)
    red_a(3, ga_live)

    col_arrive(col_pt, pt_sem, 4, (2, 3), gt_any, pt_needs)
    pa_live = x == y // 2

    @pl.when(pa_live)
    def _():
        near = sum_dots([(row_o[2 * x + k], col_la[k]) for k in (0, 1)])
        far = sum_dots([(row_o[4 + k], col_pt[k]) for k in range(4)])
        col_pa[c] = -(near + far)
        part[2] = col_pa[c] * weight

    for d in (1, 3, 2):
        xx = (x + d) % 4
        send(pa_live & (xx == y), col_pa.at[c], col_pa.at[c], pa_sem.at[c], xdev(xx))
    send(pa_live & (x == y), col_pa.at[c], col_pa.at[c], pa_sem.at[c], sib)
    red_a(2, pa_live)

    for src in (0, 1, 2, 3):
        row_arrive(row_u, ru_sem, needs_u, src)

    red_b(3, odd_live)
    red_b(2, col_live)
    red_c(3, odd_live)
    return_live = row_live
    cond = return_live & (x != 0)
    arrive(cond, col_ga.at[2 + c], ga_sem.at[c])
    send(cond, col_ga.at[2 + c], col_ga.at[2 + c], ga_sem.at[c], sib)
    arrive(return_live, col_ga.at[3 - c], ga_sem.at[1 - c])

    @pl.when(return_live & (x == 0))
    def _():
        col_ga[2 + c] = col_ga[c]

    @pl.when(row_live)
    def _():
        near = sum_dots([(row_u[2 * (x // 2) + k], col_ga[2 + k]) for k in (0, 1)])
        far = sum_dots([(row_u[4 + k], col_gt[k]) for k in range(4)])
        part[1] = -(near + far) * weight

    red_a(1, row_live)
    red_c(2, col_live)
    red_d(3, odd_live)

    cond = (x == y) & (x != y // 2)
    arrive(cond, col_pa.at[c], pa_sem.at[c])
    send(cond, col_pa.at[c], col_pa.at[c], pa_sem.at[c], sib)
    arrive(x == y, col_pa.at[1 - c], pa_sem.at[1 - c])

    @pl.when(diag_live)
    def _():
        near = sum_dots([(row_u[2 * (x // 2) + k], col_pa[k]) for k in (0, 1)])
        far = sum_dots([(row_u[4 + k], col_pt[k]) for k in range(4)])
        part[0] = (din_ref[0, even, even] - (near + far)) * weight

    red_a(0, diag_live)
    red_d(2, col_live)
    red_b(1, row_live)
    red_b(0, diag_live)
    red_c(1, row_live)
    red_c(0, diag_live)
    red_d(1, row_live)
    red_d(0, diag_live)
    red_e(3, odd_live)
    red_e(2, col_live)
    red_e(1, row_live)
    red_e(0, diag_live)

    assert len(sends) <= N_SEND
    for cond, copy in sends:
        pl.when(cond)(lambda copy=copy: copy.wait_send())


def local(lower, upper, dinv, pole_weight, block_pattern):
    vmem = pl.BlockSpec(memory_space=pltpu.VMEM)
    smem = pl.BlockSpec(memory_space=pltpu.SMEM)

    def blocks(*lead):
        return pltpu.VMEM(lead + (B, B), jnp.float32)

    def sems(*lead):
        return pltpu.SemaphoreType.DMA(lead)

    return pl.pallas_call(
        kernel,
        out_shape=jax.ShapeDtypeStruct((2 * B, 2 * B), jnp.float32),
        in_specs=[vmem, vmem, vmem, smem, smem],
        out_specs=vmem,
        scratch_shapes=[
            blocks(8), blocks(8), blocks(2), blocks(4), blocks(4), blocks(4), blocks(4), blocks(4), blocks(2),
            blocks(4), pltpu.VMEM((4, 2, 2, H, B), jnp.float32),
            sems(N_SEND), sems(8), sems(8), sems(2), sems(4), sems(4), sems(4), sems(2), sems(4), sems(2),
            sems(4, 2, 3),
        ],
        compiler_params=pltpu.CompilerParams(
            collective_id=0, has_side_effects=True, vmem_limit_bytes=48 * 2**20
        ),
    )(lower, upper, dinv, pole_weight, block_pattern)


def solution(mesh):
    in_specs = (
        P("pole", "prow", "pcol"),
        P("pole", "prow", "pcol"),
        P("pole", "prow", "pcol"),
        P("pole"),
        P(),
    )
    out_specs = P("prow", "pcol")
    return jax.shard_map(local, mesh=mesh, in_specs=in_specs, out_specs=out_specs, check_vma=False)
```

```python
import jax
import jax.numpy as jnp
from jax import lax
from jax.experimental import pallas as pl
from jax.experimental.pallas import tpu as pltpu
from jax.sharding import PartitionSpec as P

B = 256
H = B // 2
MESH = pl.DeviceIdType.MESH
N_SEND = 160


def split(values):
    high = values.astype(jnp.bfloat16)
    low = (values - high.astype(jnp.float32)).astype(jnp.bfloat16)
    return high, low


def block_dot(left, right):
    lh, ll = split(left)
    rh, rl = split(right)
    big = jnp.concatenate([lh, lh, ll], axis=1)
    tall = jnp.concatenate([rh, rl, rh], axis=0)
    return jnp.dot(big, tall, preferred_element_type=jnp.float32)


def kernel(
    low_ref, up_ref, din_ref, weight_ref, pat_ref, out_ref,
    row_o, row_u, col_la, col_lt, col_l1, col_gt, col_ga, col_pt, col_pa,
    part, inbox, raw_l, raw_d, in_sem,
    send_sem, ro_sem, ru_sem, la_sem, lt_sem, l1_sem, gt_sem, ga_sem, pt_sem, pa_sem, red_sem,
):
    p = lax.axis_index("pole")
    i = lax.axis_index("prow")
    j = lax.axis_index("pcol")
    x, c = i // 2, i % 2
    y, h = j // 2, j % 2
    sib = (p, 2 * x + 1 - c, j)
    partner = (p, i, 2 * y + 1 - h)
    jp = 2 * y + 1 - h

    def xdev(xx):
        return (p, 2 * xx + c, j)

    def ydev(yy):
        return (p, i, 2 * yy + h)

    barrier = pltpu.get_barrier_semaphore()
    others = [sib, partner]
    for d in (1, 2, 3):
        others += [xdev((x + d) % 4), ydev((y + d) % 4)]
    for dev in others:
        pl.semaphore_signal(barrier, inc=1, device_id=dev, device_id_type=MESH)

    @pl.when(p > 0)
    def _():
        pl.semaphore_signal(barrier, inc=1, device_id=(p - 1, i, j), device_id_type=MESH)

    @pl.when(p < 3)
    def _():
        pl.semaphore_signal(barrier, inc=1, device_id=(p + 1, i, j), device_id_type=MESH)

    yes = p >= 0
    sends = []

    def send(cond, src, dst, rsem, dev):
        copy = pltpu.make_async_remote_copy(
            src_ref=src, dst_ref=dst, send_sem=send_sem.at[len(sends)], recv_sem=rsem,
            device_id=dev, device_id_type=MESH,
        )
        sends.append((cond, copy))
        pl.when(cond)(lambda: copy.start())

    def arrive(cond, dst, rsem):
        copy = pltpu.make_async_remote_copy(
            src_ref=dst, dst_ref=dst, send_sem=send_sem.at[0], recv_sem=rsem,
            device_id=sib, device_id_type=MESH,
        )
        pl.when(cond)(lambda: copy.wait_recv())

    def flag(a, b):
        return jnp.where(pat_ref[a, b] > 0, 1.0, 0.0).astype(jnp.float32)

    weight = weight_ref[0]
    low_oo = flag(2 * i + 1, 2 * j + 1)
    low_oe = flag(2 * i + 1, 2 * j)
    up_oo = flag(2 * j + 1, 2 * i + 1)
    up_eo = flag(2 * j + 1, 2 * i)

    top_row = x >= 2
    top_col = y >= 2
    odd_live = top_row | top_col | (x == y)
    col_live = top_row | (x == y // 2)
    row_live = top_col | (y == x // 2)
    diag_live = x == y
    even, odd = pl.ds(0, B), pl.ds(B, B)
    minus_y = (2 * (y // 2), 2 * (y // 2) + 1)

    mid_row = ~top_row & top_col
    mid_col = top_row & ~top_col
    loads = (
        (mid_col, low_ref.at[0, odd, odd], row_o.at[j], 0),
        (mid_row, up_ref.at[0, odd, odd], row_o.at[j], 0),
        ((top_row & top_col) | (~top_row & (x == y)), din_ref.at[0, odd, odd], row_o.at[j], 0),
        (col_live, low_ref.at[0, odd, even], raw_l, 1),
        (row_live, up_ref.at[0, even, odd], row_u.at[j], 2),
        (diag_live, din_ref.at[0, even, even], raw_d, 3),
    )
    loads = [(cond, pltpu.make_async_copy(src, dst, in_sem.at[k])) for cond, src, dst, k in loads]
    for cond, copy in loads:
        pl.when(cond)(lambda copy=copy: copy.start())
    for cond, copy in loads:
        pl.when(cond)(lambda copy=copy: copy.wait())

    @pl.when(mid_col)
    def _():
        block = row_o[j] * low_oo
        row_o[j] = block
        col_l1[i - 4] = block

    @pl.when(top_row & top_col)
    def _():
        col_gt[i - 4] = row_o[j]

    @pl.when(mid_row)
    def _():
        row_o[j] = row_o[j] * up_oo

    @pl.when(col_live)
    def _():
        raw_l[...] = raw_l[...] * low_oe

    @pl.when(x == y // 2)
    def _():
        col_la[c] = raw_l[...]

    @pl.when(row_live)
    def _():
        row_u[j] = row_u[j] * up_eo

    pl.semaphore_wait(barrier, jnp.where((p == 0) | (p == 3), 9, 10))

    def needs_o(src, dst):
        wide = jnp.where(x == 1, dst >= 1, yes)
        return (((src >= 2) & wide) | ((src < 2) & (dst // 2 == src))) & (top_row | (src >= 2) | (src == x))

    def needs_u(src, dst):
        live = (src >= 2) | (src == x // 2)
        return live & ((dst >= 2) | (dst == x // 2) | (dst == x))

    def row_send(buf, sem, needs, slot):
        for d in (1, 3, 2):
            yy = (y + d) % 4
            send(needs(y, yy), buf.at[slot], buf.at[slot], sem.at[slot], ydev(yy))

    def row_arrive(buf, sem, needs, src):
        cond = needs(src, y) & (src != y)
        for half in (0, 1):
            slot = 2 * src + half
            arrive(cond, buf.at[slot], sem.at[slot])

    def col_send(buf, sem, base, live, needs):
        slot = i - base
        slot = jnp.where(live, slot, 0)
        for d in (1, 3, 2):
            xx = (x + d) % 4
            send(live & needs(xx), buf.at[slot], buf.at[slot], sem.at[slot], xdev(xx))
        send(live & needs(x), buf.at[slot], buf.at[slot], sem.at[slot], sib)

    def col_arrive(buf, sem, base, xs, live, needs):
        for xx in xs:
            near = 2 * xx + c - base
            far = 2 * xx + 1 - c - base
            cond = live(xx) & needs(x) & (xx != x)
            arrive(cond, buf.at[near], sem.at[near])
            send(cond, buf.at[near], buf.at[near], sem.at[near], sib)
        for xx in xs:
            far = 2 * xx + 1 - c - base
            arrive(live(xx) & needs(x), buf.at[far], sem.at[far])

    halves = ((0, p), (1, 3 - p))

    def toward(q, half):
        pole = q if half == 0 else 3 - q
        return (pole, i, j)

    def rows_of(quad, half):
        return pl.ds((quad // 2) * B + half * H, H), pl.ds((quad % 2) * B, B)

    def red_a(quad, live):
        for half, q in halves:
            src = part.at[quad, pl.ds(half * H, H)]
            send(live & (q == 0), src, inbox.at[quad, half, 0], red_sem.at[quad, half, 0], toward(1, half))
            send(live & (q == 3), src, inbox.at[quad, half, 1], red_sem.at[quad, half, 1], toward(2, half))

    def red_b(quad, live):
        for half, q in halves:
            arrive(live & (q == 2), inbox.at[quad, half, 1], red_sem.at[quad, half, 1])
            rows = pl.ds(half * H, H)

            @pl.when(live & (q == 2))
            def _():
                part[quad, rows] = part[quad, rows] + inbox[quad, half, 1]

            src = part.at[quad, rows]
            send(live & (q == 2), src, inbox.at[quad, half, 1], red_sem.at[quad, half, 1], toward(1, half))

    def red_c(quad, live):
        for half, q in halves:
            arrive(live & (q == 1), inbox.at[quad, half, 0], red_sem.at[quad, half, 0])
            arrive(live & (q == 1), inbox.at[quad, half, 1], red_sem.at[quad, half, 1])
            rows = pl.ds(half * H, H)
            orow, ocol = rows_of(quad, half)

            @pl.when(live & (q == 1))
            def _():
                out_ref[orow, ocol] = part[quad, rows] + inbox[quad, half, 0] + inbox[quad, half, 1]

            place = out_ref.at[orow, ocol]
            send(live & (q == 1), place, place, red_sem.at[quad, half, 2], toward(2, half))
            send(live & (q == 1), place, place, red_sem.at[quad, half, 2], toward(0, half))

    def red_d(quad, live):
        for half, q in halves:
            place = out_ref.at[rows_of(quad, half)]
            arrive(live & (q == 2), place, red_sem.at[quad, half, 2])
            send(live & (q == 2), place, place, red_sem.at[quad, half, 2], toward(3, half))

    def red_e(quad, live):
        for half, q in halves:
            place = out_ref.at[rows_of(quad, half)]
            arrive(live & ((q == 0) | (q == 3)), place, red_sem.at[quad, half, 2])

    def sum_dots(pairs):
        total = None
        for left, right in pairs:
            term = block_dot(left, right)
            total = term if total is None else total + term
        return total

    send(odd_live, row_o.at[j], row_o.at[j], ro_sem.at[j], partner)
    row_send(row_o, ro_sem, needs_o, j)
    la_live = x == y // 2
    la_needs = lambda xx: (xx >= 2) | (xx == y // 2)
    col_send(col_la, la_sem, 2 * (y // 2), la_live, la_needs)
    l1_live = top_row & ~top_col
    l1_needs = lambda xx: (xx >= 2) & (y < 2)
    col_send(col_l1, l1_sem, 4, l1_live, l1_needs)
    gt_needs = lambda xx: (y >= 2) | (xx // 2 == y) | ((xx == 1) & (y == 1))
    gt_any = lambda xx: xx >= 2
    tt = top_row & top_col
    col_send(col_gt, gt_sem, 4, tt, gt_needs)

    @pl.when(tt)
    def _():
        part[3] = row_o[j] * weight

    @pl.when(~odd_live)
    def _():
        out_ref[odd, odd] = jnp.zeros((B, B), jnp.float32)

    @pl.when(~col_live)
    def _():
        out_ref[odd, even] = jnp.zeros((B, B), jnp.float32)

    @pl.when(~row_live)
    def _():
        out_ref[even, odd] = jnp.zeros((B, B), jnp.float32)

    @pl.when(~diag_live)
    def _():
        out_ref[even, even] = jnp.zeros((B, B), jnp.float32)

    arrive(odd_live, row_o.at[jp], ro_sem.at[jp])
    row_send(row_o, ro_sem, needs_o, jp)
    send(row_live, row_u.at[j], row_u.at[j], ru_sem.at[j], partner)
    row_send(row_u, ru_sem, needs_u, j)
    red_a(3, tt)

    la_any = lambda xx: yes
    for shift in (0,):
        xx = y // 2
        near, far = c, 1 - c
        cond = la_needs(x) & (x != xx)
        arrive(cond, col_la.at[near], la_sem.at[near])
        send(cond, col_la.at[near], col_la.at[near], la_sem.at[near], sib)
        arrive(la_needs(x), col_la.at[far], la_sem.at[far])
    col_arrive(col_l1, l1_sem, 4, (2, 3), lambda xx: yes, l1_needs)
    for src in (0, 1):
        row_arrive(row_o, ro_sem, needs_o, src)

    @pl.when(top_row)
    def _():
        through = sum_dots([(row_o[minus_y[k]], col_la[k]) for k in (0, 1)])
        col_lt[i - 4] = raw_l[...] - through

    lt_needs = lambda xx: xx >= 2
    col_send(col_lt, lt_sem, 4, top_row, lt_needs)
    for src in (2, 3):
        row_arrive(row_o, ro_sem, needs_o, src)

    arrive(row_live, row_u.at[jp], ru_sem.at[jp])
    row_send(row_u, ru_sem, needs_u, jp)

    @pl.when(top_row & ~top_col)
    def _():
        col_gt[i - 4] = -sum_dots([(row_o[4 + k], col_l1[k]) for k in range(4)])

    col_send(col_gt, gt_sem, 4, top_row & ~top_col, gt_needs)

    @pl.when(mid_col)
    def _():
        part[3] = col_gt[i - 4] * weight

    red_a(3, mid_col)
    col_arrive(col_lt, lt_sem, 4, (2, 3), gt_any, lt_needs)

    @pl.when(top_row)
    def _():
        col_pt[i - 4] = -sum_dots([(row_o[4 + k], col_lt[k]) for k in range(4)])
        part[2] = col_pt[i - 4] * weight

    pt_needs = lambda xx: (xx == y // 2) | (xx == y)
    col_send(col_pt, pt_sem, 4, top_row, pt_needs)
    red_a(2, top_row)
    red_b(3, tt)

    col_arrive(col_gt, gt_sem, 4, (2, 3), gt_any, gt_needs)
    ga_live = (x < 2) & (top_col | (x == y))

    @pl.when(ga_live)
    def _():
        folded = sum_dots([(row_o[4 + k], col_gt[k]) for k in range(4)])
        col_ga[c] = jnp.where(x == y, row_o[j], 0.0) - folded
        part[3] = col_ga[c] * weight

    for d in (1, 3, 2):
        xx = (x + d) % 4
        send(ga_live & (xx // 2 == x), col_ga.at[c], col_ga.at[2 + c], ga_sem.at[c], xdev(xx))
    send(ga_live & (x == 0), col_ga.at[c], col_ga.at[2 + c], ga_sem.at[c], sib)
    red_a(3, ga_live)
    red_c(3, tt)
    red_b(3, mid_col)


    col_arrive(col_pt, pt_sem, 4, (2, 3), gt_any, pt_needs)
    pa_live = x == y // 2

    @pl.when(pa_live)
    def _():
        near = sum_dots([(row_o[2 * x + k], col_la[k]) for k in (0, 1)])
        far = sum_dots([(row_o[4 + k], col_pt[k]) for k in range(4)])
        col_pa[c] = -(near + far)
        part[2] = col_pa[c] * weight

    for d in (1, 3, 2):
        xx = (x + d) % 4
        send(pa_live & (xx == y), col_pa.at[c], col_pa.at[c], pa_sem.at[c], xdev(xx))
    send(pa_live & (x == y), col_pa.at[c], col_pa.at[c], pa_sem.at[c], sib)
    red_a(2, pa_live)
    red_b(2, top_row)
    red_d(3, tt)


    for src in (0, 1, 2, 3):
        row_arrive(row_u, ru_sem, needs_u, src)


    return_live = row_live
    cond = return_live & (x != 0)
    arrive(cond, col_ga.at[2 + c], ga_sem.at[c])
    send(cond, col_ga.at[2 + c], col_ga.at[2 + c], ga_sem.at[c], sib)
    arrive(return_live, col_ga.at[3 - c], ga_sem.at[1 - c])

    @pl.when(return_live & (x == 0))
    def _():
        col_ga[2 + c] = col_ga[c]

    @pl.when(row_live)
    def _():
        near = sum_dots([(row_u[2 * (x // 2) + k], col_ga[2 + k]) for k in (0, 1)])
        far = sum_dots([(row_u[4 + k], col_gt[k]) for k in range(4)])
        part[1] = -(near + far) * weight

    red_a(1, row_live)
    red_b(3, ga_live)
    red_c(3, mid_col)
    red_c(2, top_row)
    red_b(2, pa_live)

    cond = (x == y) & (x != y // 2)
    arrive(cond, col_pa.at[c], pa_sem.at[c])
    send(cond, col_pa.at[c], col_pa.at[c], pa_sem.at[c], sib)
    arrive(x == y, col_pa.at[1 - c], pa_sem.at[1 - c])

    @pl.when(diag_live)
    def _():
        near = sum_dots([(row_u[2 * (x // 2) + k], col_pa[k]) for k in (0, 1)])
        far = sum_dots([(row_u[4 + k], col_pt[k]) for k in range(4)])
        part[0] = (raw_d[...] - (near + far)) * weight

    red_a(0, diag_live)
    red_c(3, ga_live)
    red_c(2, pa_live)
    red_d(3, mid_col)
    red_d(2, top_row)
    red_b(1, row_live)
    red_d(3, ga_live)
    red_d(2, pa_live)
    red_b(0, diag_live)
    red_c(1, row_live)
    red_c(0, diag_live)
    red_d(1, row_live)
    red_d(0, diag_live)
    red_e(3, odd_live)
    red_e(2, col_live)
    red_e(1, row_live)
    red_e(0, diag_live)

    assert len(sends) <= N_SEND
    for cond, copy in sends:
        pl.when(cond)(lambda copy=copy: copy.wait_send())


def local(lower, upper, dinv, pole_weight, block_pattern):
    vmem = pl.BlockSpec(memory_space=pltpu.VMEM)
    smem = pl.BlockSpec(memory_space=pltpu.SMEM)
    hbm = pl.BlockSpec(memory_space=pl.ANY)

    def blocks(*lead):
        return pltpu.VMEM(lead + (B, B), jnp.float32)

    def sems(*lead):
        return pltpu.SemaphoreType.DMA(lead)

    return pl.pallas_call(
        kernel,
        out_shape=jax.ShapeDtypeStruct((2 * B, 2 * B), jnp.float32),
        in_specs=[hbm, hbm, hbm, smem, smem],
        out_specs=vmem,
        scratch_shapes=[
            blocks(8), blocks(8), blocks(2), blocks(4), blocks(4), blocks(4), blocks(4), blocks(4), blocks(2),
            blocks(4), pltpu.VMEM((4, 2, 2, H, B), jnp.float32), blocks(), blocks(), sems(4),
            sems(N_SEND), sems(8), sems(8), sems(2), sems(4), sems(4), sems(4), sems(2), sems(4), sems(2),
            sems(4, 2, 3),
        ],
        compiler_params=pltpu.CompilerParams(
            collective_id=0, has_side_effects=True, vmem_limit_bytes=52 * 2**20
        ),
    )(lower, upper, dinv, pole_weight, block_pattern)


def solution(mesh):
    in_specs = (
        P("pole", "prow", "pcol"),
        P("pole", "prow", "pcol"),
        P("pole", "prow", "pcol"),
        P("pole"),
        P(),
    )
    out_specs = P("prow", "pcol")
    return jax.shard_map(local, mesh=mesh, in_specs=in_specs, out_specs=out_specs, check_vma=False)
```

```python
import jax
import jax.numpy as jnp
from jax import lax
from jax.experimental import pallas as pl
from jax.experimental.pallas import tpu as pltpu
from jax.sharding import PartitionSpec as P

B = 256
H = B // 2
MESH = pl.DeviceIdType.MESH
N_SEND = 76


def split(values):
    high = values.astype(jnp.bfloat16)
    low = (values - high.astype(jnp.float32)).astype(jnp.bfloat16)
    return high, low


def block_dot(left, right):
    lh, ll = split(left)
    rh, rl = split(right)
    big = jnp.concatenate([lh, lh, ll], axis=1)
    tall = jnp.concatenate([rh, rl, rh], axis=0)
    return jnp.dot(big, tall, preferred_element_type=jnp.float32)


def kernel(
    low_ref, up_ref, din_ref, weight_ref, pat_ref, out_ref,
    row_o, row_u, col_la, col_lt, col_l1, col_gt, col_ga, col_pt, col_pa,
    part, inbox, raw_l, raw_d, in_sem,
    send_sem, ro_sem, ru_sem, la_sem, lt_sem, l1_sem, gt_sem, ga_sem, pt_sem, pa_sem, red_sem,
):
    p = lax.axis_index("pole")
    i = lax.axis_index("prow")
    j = lax.axis_index("pcol")
    x, c = i // 2, i % 2
    y, h = j // 2, j % 2
    sib = (p, 2 * x + 1 - c, j)
    partner = (p, i, 2 * y + 1 - h)
    jp = 2 * y + 1 - h

    def xdev(xx):
        return (p, 2 * xx + c, j)

    def ydev(yy):
        return (p, i, 2 * yy + h)

    barrier = pltpu.get_barrier_semaphore()
    others = [sib, partner]
    for d in (1, 2, 3):
        others += [xdev((x + d) % 4), ydev((y + d) % 4)]
    for dev in others:
        pl.semaphore_signal(barrier, inc=1, device_id=dev, device_id_type=MESH)

    @pl.when(p > 0)
    def _():
        pl.semaphore_signal(barrier, inc=1, device_id=(p - 1, i, j), device_id_type=MESH)

    @pl.when(p < 3)
    def _():
        pl.semaphore_signal(barrier, inc=1, device_id=(p + 1, i, j), device_id_type=MESH)

    yes = p >= 0
    sends = []

    slots = {}

    def send(cond, src, dst, rsem, dev, key=None):
        slot = slots.setdefault(len(sends) if key is None else key, len(slots))
        copy = pltpu.make_async_remote_copy(
            src_ref=src, dst_ref=dst, send_sem=send_sem.at[slot], recv_sem=rsem,
            device_id=dev, device_id_type=MESH,
        )
        sends.append((cond, copy))
        pl.when(cond)(lambda: copy.start())

    def arrive(cond, dst, rsem):
        copy = pltpu.make_async_remote_copy(
            src_ref=dst, dst_ref=dst, send_sem=send_sem.at[0], recv_sem=rsem,
            device_id=sib, device_id_type=MESH,
        )
        pl.when(cond)(lambda: copy.wait_recv())

    def flag(a, b):
        return jnp.where(pat_ref[a, b] > 0, 1.0, 0.0).astype(jnp.float32)

    weight = weight_ref[0]
    low_oo = flag(2 * i + 1, 2 * j + 1)
    low_oe = flag(2 * i + 1, 2 * j)
    up_oo = flag(2 * j + 1, 2 * i + 1)
    up_eo = flag(2 * j + 1, 2 * i)

    top_row = x >= 2
    top_col = y >= 2
    odd_live = top_row | top_col | (x == y)
    col_live = top_row | (x == y // 2)
    row_live = top_col | (y == x // 2)
    diag_live = x == y
    even, odd = pl.ds(0, B), pl.ds(B, B)
    minus_y = (2 * (y // 2), 2 * (y // 2) + 1)

    mid_row = ~top_row & top_col
    mid_col = top_row & ~top_col
    loads = (
        (mid_col, low_ref.at[0, odd, odd], row_o.at[j], 0),
        (mid_row, up_ref.at[0, odd, odd], row_o.at[j], 0),
        ((top_row & top_col) | (~top_row & (x == y)), din_ref.at[0, odd, odd], row_o.at[j], 0),
        (col_live, low_ref.at[0, odd, even], raw_l, 1),
        (row_live, up_ref.at[0, even, odd], row_u.at[j], 2),
        (diag_live, din_ref.at[0, even, even], raw_d, 3),
    )
    loads = [(cond, pltpu.make_async_copy(src, dst, in_sem.at[k])) for cond, src, dst, k in loads]
    for cond, copy in loads:
        pl.when(cond)(lambda copy=copy: copy.start())
    for cond, copy in loads:
        pl.when(cond)(lambda copy=copy: copy.wait())

    @pl.when(mid_col)
    def _():
        block = row_o[j] * low_oo
        row_o[j] = block
        col_l1[i - 4] = block

    @pl.when(top_row & top_col)
    def _():
        col_gt[i - 4] = row_o[j]

    @pl.when(mid_row)
    def _():
        row_o[j] = row_o[j] * up_oo

    @pl.when(col_live)
    def _():
        raw_l[...] = raw_l[...] * low_oe

    @pl.when(x == y // 2)
    def _():
        col_la[c] = raw_l[...]

    @pl.when(row_live)
    def _():
        row_u[j] = row_u[j] * up_eo

    pl.semaphore_wait(barrier, jnp.where((p == 0) | (p == 3), 9, 10))

    def needs_o(src, dst):
        wide = jnp.where(x == 1, dst >= 1, yes)
        return (((src >= 2) & wide) | ((src < 2) & (dst // 2 == src))) & (top_row | (src >= 2) | (src == x))

    def needs_u(src, dst):
        live = (src >= 2) | (src == x // 2)
        return live & ((dst >= 2) | (dst == x // 2) | (dst == x))

    def row_send(buf, sem, needs, slot):
        for d in (1, 3, 2):
            yy = (y + d) % 4
            send(needs(y, yy), buf.at[slot], buf.at[slot], sem.at[slot], ydev(yy))

    def row_arrive(buf, sem, needs, src):
        cond = needs(src, y) & (src != y)
        for half in (0, 1):
            slot = 2 * src + half
            arrive(cond, buf.at[slot], sem.at[slot])

    def col_send(buf, sem, base, live, needs):
        slot = i - base
        slot = jnp.where(live, slot, 0)
        for d in (1, 3, 2):
            xx = (x + d) % 4
            send(live & needs(xx), buf.at[slot], buf.at[slot], sem.at[slot], xdev(xx))
        send(live & needs(x), buf.at[slot], buf.at[slot], sem.at[slot], sib)

    def col_arrive(buf, sem, base, xs, live, needs):
        for xx in xs:
            near = 2 * xx + c - base
            far = 2 * xx + 1 - c - base
            cond = live(xx) & needs(x) & (xx != x)
            arrive(cond, buf.at[near], sem.at[near])
            send(cond, buf.at[near], buf.at[near], sem.at[near], sib)
        for xx in xs:
            far = 2 * xx + 1 - c - base
            arrive(live(xx) & needs(x), buf.at[far], sem.at[far])

    halves = ((0, p), (1, 3 - p))

    def toward(q, half):
        pole = q if half == 0 else 3 - q
        return (pole, i, j)

    def rows_of(quad, half):
        return pl.ds((quad // 2) * B + half * H, H), pl.ds((quad % 2) * B, B)

    def red_a(quad, live):
        for half, q in halves:
            src = part.at[quad, pl.ds(half * H, H)]
            send(live & (q == 0), src, inbox.at[quad, half, 0], red_sem.at[quad, half, 0], toward(1, half), (quad, half))
            send(live & (q == 3), src, inbox.at[quad, half, 1], red_sem.at[quad, half, 1], toward(2, half), (quad, half))

    def red_b(quad, live):
        for half, q in halves:
            arrive(live & (q == 2), inbox.at[quad, half, 1], red_sem.at[quad, half, 1])
            rows = pl.ds(half * H, H)

            @pl.when(live & (q == 2))
            def _():
                part[quad, rows] = part[quad, rows] + inbox[quad, half, 1]

            src = part.at[quad, rows]
            send(live & (q == 2), src, inbox.at[quad, half, 1], red_sem.at[quad, half, 1], toward(1, half), (quad, half))

    def red_c(quad, live):
        for half, q in halves:
            arrive(live & (q == 1), inbox.at[quad, half, 0], red_sem.at[quad, half, 0])
            arrive(live & (q == 1), inbox.at[quad, half, 1], red_sem.at[quad, half, 1])
            rows = pl.ds(half * H, H)
            orow, ocol = rows_of(quad, half)

            @pl.when(live & (q == 1))
            def _():
                out_ref[orow, ocol] = part[quad, rows] + inbox[quad, half, 0] + inbox[quad, half, 1]

            place = out_ref.at[orow, ocol]
            send(live & (q == 1), place, place, red_sem.at[quad, half, 2], toward(2, half), (quad, half))
            send(live & (q == 1), place, place, red_sem.at[quad, half, 2], toward(0, half), (quad, half, 2))

    def red_d(quad, live):
        for half, q in halves:
            place = out_ref.at[rows_of(quad, half)]
            arrive(live & (q == 2), place, red_sem.at[quad, half, 2])
            send(live & (q == 2), place, place, red_sem.at[quad, half, 2], toward(3, half), (quad, half, 2))

    def red_e(quad, live):
        for half, q in halves:
            place = out_ref.at[rows_of(quad, half)]
            arrive(live & ((q == 0) | (q == 3)), place, red_sem.at[quad, half, 2])

    def sum_dots(pairs):
        total = None
        for left, right in pairs:
            term = block_dot(left, right)
            total = term if total is None else total + term
        return total

    send(odd_live, row_o.at[j], row_o.at[j], ro_sem.at[j], partner)
    row_send(row_o, ro_sem, needs_o, j)
    la_live = x == y // 2
    la_needs = lambda xx: (xx >= 2) | (xx == y // 2)
    col_send(col_la, la_sem, 2 * (y // 2), la_live, la_needs)
    l1_live = top_row & ~top_col
    l1_needs = lambda xx: (xx >= 2) & (y < 2)
    col_send(col_l1, l1_sem, 4, l1_live, l1_needs)
    gt_needs = lambda xx: (y >= 2) | (xx // 2 == y) | ((xx == 1) & (y == 1))
    gt_any = lambda xx: xx >= 2
    tt = top_row & top_col
    col_send(col_gt, gt_sem, 4, tt, gt_needs)

    @pl.when(tt)
    def _():
        part[3] = row_o[j] * weight

    @pl.when(~odd_live)
    def _():
        out_ref[odd, odd] = jnp.zeros((B, B), jnp.float32)

    @pl.when(~col_live)
    def _():
        out_ref[odd, even] = jnp.zeros((B, B), jnp.float32)

    @pl.when(~row_live)
    def _():
        out_ref[even, odd] = jnp.zeros((B, B), jnp.float32)

    @pl.when(~diag_live)
    def _():
        out_ref[even, even] = jnp.zeros((B, B), jnp.float32)

    arrive(odd_live, row_o.at[jp], ro_sem.at[jp])
    row_send(row_o, ro_sem, needs_o, jp)
    send(row_live, row_u.at[j], row_u.at[j], ru_sem.at[j], partner)
    row_send(row_u, ru_sem, needs_u, j)
    red_a(3, tt)

    la_any = lambda xx: yes
    for shift in (0,):
        xx = y // 2
        near, far = c, 1 - c
        cond = la_needs(x) & (x != xx)
        arrive(cond, col_la.at[near], la_sem.at[near])
        send(cond, col_la.at[near], col_la.at[near], la_sem.at[near], sib)
        arrive(la_needs(x), col_la.at[far], la_sem.at[far])
    col_arrive(col_l1, l1_sem, 4, (2, 3), lambda xx: yes, l1_needs)
    for src in (0, 1):
        row_arrive(row_o, ro_sem, needs_o, src)

    @pl.when(top_row)
    def _():
        through = sum_dots([(row_o[minus_y[k]], col_la[k]) for k in (0, 1)])
        col_lt[i - 4] = raw_l[...] - through

    lt_needs = lambda xx: xx >= 2
    col_send(col_lt, lt_sem, 4, top_row, lt_needs)
    for src in (2, 3):
        row_arrive(row_o, ro_sem, needs_o, src)

    arrive(row_live, row_u.at[jp], ru_sem.at[jp])
    row_send(row_u, ru_sem, needs_u, jp)

    @pl.when(top_row & ~top_col)
    def _():
        col_gt[i - 4] = -sum_dots([(row_o[4 + k], col_l1[k]) for k in range(4)])

    col_send(col_gt, gt_sem, 4, top_row & ~top_col, gt_needs)

    @pl.when(mid_col)
    def _():
        part[3] = col_gt[i - 4] * weight

    red_a(3, mid_col)
    col_arrive(col_lt, lt_sem, 4, (2, 3), gt_any, lt_needs)

    @pl.when(top_row)
    def _():
        col_pt[i - 4] = -sum_dots([(row_o[4 + k], col_lt[k]) for k in range(4)])
        part[2] = col_pt[i - 4] * weight

    pt_needs = lambda xx: (xx == y // 2) | (xx == y)
    col_send(col_pt, pt_sem, 4, top_row, pt_needs)
    red_a(2, top_row)
    red_b(3, tt)

    col_arrive(col_gt, gt_sem, 4, (2, 3), gt_any, gt_needs)
    ga_live = (x < 2) & (top_col | (x == y))

    @pl.when(ga_live)
    def _():
        folded = sum_dots([(row_o[4 + k], col_gt[k]) for k in range(4)])
        col_ga[c] = jnp.where(x == y, row_o[j], 0.0) - folded
        part[3] = col_ga[c] * weight

    for d in (1, 3, 2):
        xx = (x + d) % 4
        send(ga_live & (xx // 2 == x), col_ga.at[c], col_ga.at[2 + c], ga_sem.at[c], xdev(xx))
    send(ga_live & (x == 0), col_ga.at[c], col_ga.at[2 + c], ga_sem.at[c], sib)
    red_a(3, ga_live)
    red_c(3, tt)
    red_b(3, mid_col)


    col_arrive(col_pt, pt_sem, 4, (2, 3), gt_any, pt_needs)
    pa_live = x == y // 2

    @pl.when(pa_live)
    def _():
        near = sum_dots([(row_o[2 * x + k], col_la[k]) for k in (0, 1)])
        far = sum_dots([(row_o[4 + k], col_pt[k]) for k in range(4)])
        col_pa[c] = -(near + far)
        part[2] = col_pa[c] * weight

    for d in (1, 3, 2):
        xx = (x + d) % 4
        send(pa_live & (xx == y), col_pa.at[c], col_pa.at[c], pa_sem.at[c], xdev(xx))
    send(pa_live & (x == y), col_pa.at[c], col_pa.at[c], pa_sem.at[c], sib)
    red_a(2, pa_live)
    red_b(2, top_row)
    red_d(3, tt)


    for src in (0, 1, 2, 3):
        row_arrive(row_u, ru_sem, needs_u, src)


    return_live = row_live
    cond = return_live & (x != 0)
    arrive(cond, col_ga.at[2 + c], ga_sem.at[c])
    send(cond, col_ga.at[2 + c], col_ga.at[2 + c], ga_sem.at[c], sib)
    arrive(return_live, col_ga.at[3 - c], ga_sem.at[1 - c])

    @pl.when(return_live & (x == 0))
    def _():
        col_ga[2 + c] = col_ga[c]

    @pl.when(row_live)
    def _():
        near = sum_dots([(row_u[2 * (x // 2) + k], col_ga[2 + k]) for k in (0, 1)])
        far = sum_dots([(row_u[4 + k], col_gt[k]) for k in range(4)])
        part[1] = -(near + far) * weight

    red_a(1, row_live)
    red_b(3, ga_live)
    red_c(3, mid_col)
    red_c(2, top_row)
    red_b(2, pa_live)

    cond = (x == y) & (x != y // 2)
    arrive(cond, col_pa.at[c], pa_sem.at[c])
    send(cond, col_pa.at[c], col_pa.at[c], pa_sem.at[c], sib)
    arrive(x == y, col_pa.at[1 - c], pa_sem.at[1 - c])

    @pl.when(diag_live)
    def _():
        near = sum_dots([(row_u[2 * (x // 2) + k], col_pa[k]) for k in (0, 1)])
        far = sum_dots([(row_u[4 + k], col_pt[k]) for k in range(4)])
        part[0] = (raw_d[...] - (near + far)) * weight

    red_a(0, diag_live)
    red_c(3, ga_live)
    red_c(2, pa_live)
    red_d(3, mid_col)
    red_d(2, top_row)
    red_b(1, row_live)
    red_d(3, ga_live)
    red_d(2, pa_live)
    red_b(0, diag_live)
    red_c(1, row_live)
    red_c(0, diag_live)
    red_d(1, row_live)
    red_d(0, diag_live)
    red_e(3, odd_live)
    red_e(2, col_live)
    red_e(1, row_live)
    red_e(0, diag_live)

    assert len(slots) <= N_SEND
    for cond, copy in sends:
        pl.when(cond)(lambda copy=copy: copy.wait_send())


def local(lower, upper, dinv, pole_weight, block_pattern):
    vmem = pl.BlockSpec(memory_space=pltpu.VMEM)
    smem = pl.BlockSpec(memory_space=pltpu.SMEM)
    hbm = pl.BlockSpec(memory_space=pl.ANY)

    def blocks(*lead):
        return pltpu.VMEM(lead + (B, B), jnp.float32)

    def sems(*lead):
        return pltpu.SemaphoreType.DMA(lead)

    return pl.pallas_call(
        kernel,
        out_shape=jax.ShapeDtypeStruct((2 * B, 2 * B), jnp.float32),
        in_specs=[hbm, hbm, hbm, smem, smem],
        out_specs=vmem,
        scratch_shapes=[
            blocks(8), blocks(8), blocks(2), blocks(4), blocks(4), blocks(4), blocks(4), blocks(4), blocks(2),
            blocks(4), pltpu.VMEM((4, 2, 2, H, B), jnp.float32), blocks(), blocks(), sems(4),
            sems(N_SEND), sems(8), sems(8), sems(2), sems(4), sems(4), sems(4), sems(2), sems(4), sems(2),
            sems(4, 2, 3),
        ],
        compiler_params=pltpu.CompilerParams(
            collective_id=0, has_side_effects=True, vmem_limit_bytes=52 * 2**20
        ),
    )(lower, upper, dinv, pole_weight, block_pattern)


def solution(mesh):
    in_specs = (
        P("pole", "prow", "pcol"),
        P("pole", "prow", "pcol"),
        P("pole", "prow", "pcol"),
        P("pole"),
        P(),
    )
    out_specs = P("prow", "pcol")
    return jax.shard_map(local, mesh=mesh, in_specs=in_specs, out_specs=out_specs, check_vma=False)
```

```python
import jax
import jax.numpy as jnp
from jax import lax
from jax.experimental import pallas as pl
from jax.experimental.pallas import tpu as pltpu
from jax.sharding import PartitionSpec as P

B = 256
H = B // 2
MESH = pl.DeviceIdType.MESH
N_SEND = 76


def split(values):
    high = values.astype(jnp.bfloat16)
    low = (values - high.astype(jnp.float32)).astype(jnp.bfloat16)
    return high, low


def block_dot(left, right):
    lh, ll = split(left)
    rh, rl = split(right)
    big = jnp.concatenate([lh, lh, ll], axis=1)
    tall = jnp.concatenate([rh, rl, rh], axis=0)
    return jnp.dot(big, tall, preferred_element_type=jnp.float32)


def kernel(
    low_ref, up_ref, din_ref, weight_ref, pat_ref, out_ref,
    row_o, row_u, col_la, col_lt, col_l1, col_gt, col_ga, col_pt, col_pa,
    part, inbox, raw_l, raw_d, in_sem,
    send_sem, ro_sem, ru_sem, la_sem, lt_sem, l1_sem, gt_sem, ga_sem, pt_sem, pa_sem, red_sem,
):
    p = lax.axis_index("pole")
    i = lax.axis_index("prow")
    j = lax.axis_index("pcol")
    x, c = i // 2, i % 2
    y, h = j // 2, j % 2
    sib = (p, 2 * x + 1 - c, j)
    partner = (p, i, 2 * y + 1 - h)
    jp = 2 * y + 1 - h

    def xdev(xx):
        return (p, 2 * xx + c, j)

    def ydev(yy):
        return (p, i, 2 * yy + h)

    barrier = pltpu.get_barrier_semaphore()
    others = [sib, partner]
    for d in (1, 2, 3):
        others += [xdev((x + d) % 4), ydev((y + d) % 4)]
    for dev in others:
        pl.semaphore_signal(barrier, inc=1, device_id=dev, device_id_type=MESH)

    @pl.when(p > 0)
    def _():
        pl.semaphore_signal(barrier, inc=1, device_id=(p - 1, i, j), device_id_type=MESH)

    @pl.when(p < 3)
    def _():
        pl.semaphore_signal(barrier, inc=1, device_id=(p + 1, i, j), device_id_type=MESH)

    yes = p >= 0
    sends = []

    slots = {}

    def send(cond, src, dst, rsem, dev, key=None):
        slot = slots.setdefault(len(sends) if key is None else key, len(slots))
        copy = pltpu.make_async_remote_copy(
            src_ref=src, dst_ref=dst, send_sem=send_sem.at[slot], recv_sem=rsem,
            device_id=dev, device_id_type=MESH,
        )
        sends.append((cond, copy))
        pl.when(cond)(lambda: copy.start())

    def arrive(cond, dst, rsem):
        copy = pltpu.make_async_remote_copy(
            src_ref=dst, dst_ref=dst, send_sem=send_sem.at[0], recv_sem=rsem,
            device_id=sib, device_id_type=MESH,
        )
        pl.when(cond)(lambda: copy.wait_recv())

    def flag(a, b):
        return jnp.where(pat_ref[a, b] > 0, 1.0, 0.0).astype(jnp.float32)

    weight = weight_ref[0]
    low_oo = flag(2 * i + 1, 2 * j + 1)
    low_oe = flag(2 * i + 1, 2 * j)
    up_oo = flag(2 * j + 1, 2 * i + 1)
    up_eo = flag(2 * j + 1, 2 * i)

    top_row = x >= 2
    top_col = y >= 2
    odd_live = top_row | top_col | (x == y)
    col_live = top_row | (x == y // 2)
    row_live = top_col | (y == x // 2)
    diag_live = x == y
    even, odd = pl.ds(0, B), pl.ds(B, B)
    minus_y = (2 * (y // 2), 2 * (y // 2) + 1)

    mid_row = ~top_row & top_col
    mid_col = top_row & ~top_col
    loads = (
        (mid_col, low_ref.at[0, odd, odd], row_o.at[j], 0),
        (mid_row, up_ref.at[0, odd, odd], row_o.at[j], 0),
        ((top_row & top_col) | (~top_row & (x == y)), din_ref.at[0, odd, odd], row_o.at[j], 0),
        (col_live, low_ref.at[0, odd, even], raw_l, 1),
        (row_live, up_ref.at[0, even, odd], row_u.at[j], 2),
        (diag_live, din_ref.at[0, even, even], raw_d, 3),
    )
    loads = [(cond, pltpu.make_async_copy(src, dst, in_sem.at[k])) for cond, src, dst, k in loads]
    for cond, copy in loads:
        pl.when(cond)(lambda copy=copy: copy.start())
    for cond, copy in loads:
        pl.when(cond)(lambda copy=copy: copy.wait())

    @pl.when(mid_col)
    def _():
        block = row_o[j] * low_oo
        row_o[j] = block
        col_l1[i - 4] = block

    @pl.when(top_row & top_col)
    def _():
        col_gt[i - 4] = row_o[j]

    @pl.when(mid_row)
    def _():
        row_o[j] = row_o[j] * up_oo

    @pl.when(col_live)
    def _():
        raw_l[...] = raw_l[...] * low_oe

    @pl.when(x == y // 2)
    def _():
        col_la[c] = raw_l[...]

    @pl.when(row_live)
    def _():
        row_u[j] = row_u[j] * up_eo

    pl.semaphore_wait(barrier, jnp.where((p == 0) | (p == 3), 9, 10))

    def needs_o(src, dst):
        wide = jnp.where(x == 1, dst >= 1, yes)
        return (((src >= 2) & wide) | ((src < 2) & (dst // 2 == src))) & (top_row | (src >= 2) | (src == x))

    def needs_u(src, dst):
        live = (src >= 2) | (src == x // 2)
        return live & ((dst >= 2) | (dst == x // 2) | (dst == x))

    def row_send(buf, sem, needs, slot):
        for d in (1, 3, 2):
            yy = (y + d) % 4
            send(needs(y, yy), buf.at[slot], buf.at[slot], sem.at[slot], ydev(yy))

    def row_arrive(buf, sem, needs, src):
        cond = needs(src, y) & (src != y)
        for half in (0, 1):
            slot = 2 * src + half
            arrive(cond, buf.at[slot], sem.at[slot])

    def col_send(buf, sem, base, live, needs):
        slot = i - base
        slot = jnp.where(live, slot, 0)
        for d in (1, 3, 2):
            xx = (x + d) % 4
            send(live & needs(xx), buf.at[slot], buf.at[slot], sem.at[slot], xdev(xx))
        send(live & needs(x), buf.at[slot], buf.at[slot], sem.at[slot], sib)

    def col_arrive(buf, sem, base, xs, live, needs):
        for xx in xs:
            near = 2 * xx + c - base
            far = 2 * xx + 1 - c - base
            cond = live(xx) & needs(x) & (xx != x)
            arrive(cond, buf.at[near], sem.at[near])
            send(cond, buf.at[near], buf.at[near], sem.at[near], sib)
        for xx in xs:
            far = 2 * xx + 1 - c - base
            arrive(live(xx) & needs(x), buf.at[far], sem.at[far])

    halves = ((0, p), (1, 3 - p))

    def toward(q, half):
        pole = q if half == 0 else 3 - q
        return (pole, i, j)

    def rows_of(quad, half):
        return pl.ds((quad // 2) * B + half * H, H), pl.ds((quad % 2) * B, B)

    def red_a(quad, live):
        for half, q in halves:
            src = part.at[quad, pl.ds(half * H, H)]
            send(live & (q == 0), src, inbox.at[quad, half, 0], red_sem.at[quad, half, 0], toward(1, half), (quad, half))
            send(live & (q == 3), src, inbox.at[quad, half, 1], red_sem.at[quad, half, 1], toward(2, half), (quad, half))

    def red_b(quad, live):
        for half, q in halves:
            arrive(live & (q == 2), inbox.at[quad, half, 1], red_sem.at[quad, half, 1])
            rows = pl.ds(half * H, H)

            @pl.when(live & (q == 2))
            def _():
                part[quad, rows] = part[quad, rows] + inbox[quad, half, 1]

            src = part.at[quad, rows]
            send(live & (q == 2), src, inbox.at[quad, half, 1], red_sem.at[quad, half, 1], toward(1, half), (quad, half))

    def red_c(quad, live):
        for half, q in halves:
            arrive(live & (q == 1), inbox.at[quad, half, 0], red_sem.at[quad, half, 0])
            arrive(live & (q == 1), inbox.at[quad, half, 1], red_sem.at[quad, half, 1])
            rows = pl.ds(half * H, H)
            orow, ocol = rows_of(quad, half)

            @pl.when(live & (q == 1))
            def _():
                out_ref[orow, ocol] = part[quad, rows] + inbox[quad, half, 0] + inbox[quad, half, 1]

            place = out_ref.at[orow, ocol]
            send(live & (q == 1), place, place, red_sem.at[quad, half, 2], toward(2, half), (quad, half))
            send(live & (q == 1), place, place, red_sem.at[quad, half, 2], toward(0, half), (quad, half, 2))

    def red_d(quad, live):
        for half, q in halves:
            place = out_ref.at[rows_of(quad, half)]
            arrive(live & (q == 2), place, red_sem.at[quad, half, 2])
            send(live & (q == 2), place, place, red_sem.at[quad, half, 2], toward(3, half), (quad, half, 2))

    def red_e(quad, live):
        for half, q in halves:
            place = out_ref.at[rows_of(quad, half)]
            arrive(live & ((q == 0) | (q == 3)), place, red_sem.at[quad, half, 2])

    def sum_dots(pairs):
        total = None
        for left, right in pairs:
            term = block_dot(left, right)
            total = term if total is None else total + term
        return total

    send(odd_live, row_o.at[j], row_o.at[j], ro_sem.at[j], partner)
    row_send(row_o, ro_sem, needs_o, j)
    la_live = x == y // 2
    la_needs = lambda xx: (xx >= 2) | (xx == y // 2)
    col_send(col_la, la_sem, 2 * (y // 2), la_live, la_needs)
    l1_live = top_row & ~top_col
    l1_needs = lambda xx: (xx >= 2) & (y < 2)
    col_send(col_l1, l1_sem, 4, l1_live, l1_needs)
    gt_needs = lambda xx: (y >= 2) | (xx // 2 == y) | ((xx == 1) & (y == 1))
    gt_any = lambda xx: xx >= 2
    tt = top_row & top_col
    col_send(col_gt, gt_sem, 4, tt, gt_needs)

    @pl.when(tt)
    def _():
        part[3] = row_o[j] * weight

    @pl.when(~odd_live)
    def _():
        out_ref[odd, odd] = jnp.zeros((B, B), jnp.float32)

    @pl.when(~col_live)
    def _():
        out_ref[odd, even] = jnp.zeros((B, B), jnp.float32)

    @pl.when(~row_live)
    def _():
        out_ref[even, odd] = jnp.zeros((B, B), jnp.float32)

    @pl.when(~diag_live)
    def _():
        out_ref[even, even] = jnp.zeros((B, B), jnp.float32)

    arrive(odd_live, row_o.at[jp], ro_sem.at[jp])
    row_send(row_o, ro_sem, needs_o, jp)
    send(row_live, row_u.at[j], row_u.at[j], ru_sem.at[j], partner)
    red_a(3, tt)

    la_any = lambda xx: yes
    for shift in (0,):
        xx = y // 2
        near, far = c, 1 - c
        cond = la_needs(x) & (x != xx)
        arrive(cond, col_la.at[near], la_sem.at[near])
        send(cond, col_la.at[near], col_la.at[near], la_sem.at[near], sib)
        arrive(la_needs(x), col_la.at[far], la_sem.at[far])
    col_arrive(col_l1, l1_sem, 4, (2, 3), lambda xx: yes, l1_needs)
    for src in (0, 1):
        row_arrive(row_o, ro_sem, needs_o, src)

    @pl.when(top_row)
    def _():
        through = sum_dots([(row_o[minus_y[k]], col_la[k]) for k in (0, 1)])
        col_lt[i - 4] = raw_l[...] - through

    lt_needs = lambda xx: xx >= 2
    col_send(col_lt, lt_sem, 4, top_row, lt_needs)
    for src in (2, 3):
        row_arrive(row_o, ro_sem, needs_o, src)

    row_send(row_u, ru_sem, needs_u, j)
    arrive(row_live, row_u.at[jp], ru_sem.at[jp])
    row_send(row_u, ru_sem, needs_u, jp)

    @pl.when(top_row & ~top_col)
    def _():
        col_gt[i - 4] = -sum_dots([(row_o[4 + k], col_l1[k]) for k in range(4)])

    col_send(col_gt, gt_sem, 4, top_row & ~top_col, gt_needs)

    @pl.when(mid_col)
    def _():
        part[3] = col_gt[i - 4] * weight

    red_a(3, mid_col)
    col_arrive(col_lt, lt_sem, 4, (2, 3), gt_any, lt_needs)

    @pl.when(top_row)
    def _():
        col_pt[i - 4] = -sum_dots([(row_o[4 + k], col_lt[k]) for k in range(4)])
        part[2] = col_pt[i - 4] * weight

    pt_needs = lambda xx: (xx == y // 2) | (xx == y)
    col_send(col_pt, pt_sem, 4, top_row, pt_needs)
    red_a(2, top_row)
    red_b(3, tt)

    col_arrive(col_gt, gt_sem, 4, (2, 3), gt_any, gt_needs)
    ga_live = (x < 2) & (top_col | (x == y))

    @pl.when(ga_live)
    def _():
        folded = sum_dots([(row_o[4 + k], col_gt[k]) for k in range(4)])
        col_ga[c] = jnp.where(x == y, row_o[j], 0.0) - folded
        part[3] = col_ga[c] * weight

    for d in (1, 3, 2):
        xx = (x + d) % 4
        send(ga_live & (xx // 2 == x), col_ga.at[c], col_ga.at[2 + c], ga_sem.at[c], xdev(xx))
    send(ga_live & (x == 0), col_ga.at[c], col_ga.at[2 + c], ga_sem.at[c], sib)
    red_a(3, ga_live)
    red_c(3, tt)
    red_b(3, mid_col)


    col_arrive(col_pt, pt_sem, 4, (2, 3), gt_any, pt_needs)
    pa_live = x == y // 2

    @pl.when(pa_live)
    def _():
        near = sum_dots([(row_o[2 * x + k], col_la[k]) for k in (0, 1)])
        far = sum_dots([(row_o[4 + k], col_pt[k]) for k in range(4)])
        col_pa[c] = -(near + far)
        part[2] = col_pa[c] * weight

    for d in (1, 3, 2):
        xx = (x + d) % 4
        send(pa_live & (xx == y), col_pa.at[c], col_pa.at[c], pa_sem.at[c], xdev(xx))
    send(pa_live & (x == y), col_pa.at[c], col_pa.at[c], pa_sem.at[c], sib)
    red_a(2, pa_live)
    red_b(2, top_row)
    red_d(3, tt)


    for src in (0, 1, 2, 3):
        row_arrive(row_u, ru_sem, needs_u, src)


    return_live = row_live
    cond = return_live & (x != 0)
    arrive(cond, col_ga.at[2 + c], ga_sem.at[c])
    send(cond, col_ga.at[2 + c], col_ga.at[2 + c], ga_sem.at[c], sib)
    arrive(return_live, col_ga.at[3 - c], ga_sem.at[1 - c])

    @pl.when(return_live & (x == 0))
    def _():
        col_ga[2 + c] = col_ga[c]

    @pl.when(row_live)
    def _():
        near = sum_dots([(row_u[2 * (x // 2) + k], col_ga[2 + k]) for k in (0, 1)])
        far = sum_dots([(row_u[4 + k], col_gt[k]) for k in range(4)])
        part[1] = -(near + far) * weight

    red_a(1, row_live)
    red_b(3, ga_live)
    red_c(3, mid_col)
    red_c(2, top_row)
    red_b(2, pa_live)

    cond = (x == y) & (x != y // 2)
    arrive(cond, col_pa.at[c], pa_sem.at[c])
    send(cond, col_pa.at[c], col_pa.at[c], pa_sem.at[c], sib)
    arrive(x == y, col_pa.at[1 - c], pa_sem.at[1 - c])

    @pl.when(diag_live)
    def _():
        near = sum_dots([(row_u[2 * (x // 2) + k], col_pa[k]) for k in (0, 1)])
        far = sum_dots([(row_u[4 + k], col_pt[k]) for k in range(4)])
        part[0] = (raw_d[...] - (near + far)) * weight

    red_a(0, diag_live)
    red_c(3, ga_live)
    red_c(2, pa_live)
    red_d(3, mid_col)
    red_d(2, top_row)
    red_b(1, row_live)
    red_d(3, ga_live)
    red_d(2, pa_live)
    red_b(0, diag_live)
    red_c(1, row_live)
    red_c(0, diag_live)
    red_d(1, row_live)
    red_d(0, diag_live)
    red_e(3, odd_live)
    red_e(2, col_live)
    red_e(1, row_live)
    red_e(0, diag_live)

    assert len(slots) <= N_SEND
    for cond, copy in sends:
        pl.when(cond)(lambda copy=copy: copy.wait_send())


def local(lower, upper, dinv, pole_weight, block_pattern):
    vmem = pl.BlockSpec(memory_space=pltpu.VMEM)
    smem = pl.BlockSpec(memory_space=pltpu.SMEM)
    hbm = pl.BlockSpec(memory_space=pl.ANY)

    def blocks(*lead):
        return pltpu.VMEM(lead + (B, B), jnp.float32)

    def sems(*lead):
        return pltpu.SemaphoreType.DMA(lead)

    return pl.pallas_call(
        kernel,
        out_shape=jax.ShapeDtypeStruct((2 * B, 2 * B), jnp.float32),
        in_specs=[hbm, hbm, hbm, smem, smem],
        out_specs=vmem,
        scratch_shapes=[
            blocks(8), blocks(8), blocks(2), blocks(4), blocks(4), blocks(4), blocks(4), blocks(4), blocks(2),
            blocks(4), pltpu.VMEM((4, 2, 2, H, B), jnp.float32), blocks(), blocks(), sems(4),
            sems(N_SEND), sems(8), sems(8), sems(2), sems(4), sems(4), sems(4), sems(2), sems(4), sems(2),
            sems(4, 2, 3),
        ],
        compiler_params=pltpu.CompilerParams(
            collective_id=0, has_side_effects=True, vmem_limit_bytes=52 * 2**20
        ),
    )(lower, upper, dinv, pole_weight, block_pattern)


def solution(mesh):
    in_specs = (
        P("pole", "prow", "pcol"),
        P("pole", "prow", "pcol"),
        P("pole", "prow", "pcol"),
        P("pole"),
        P(),
    )
    out_specs = P("prow", "pcol")
    return jax.shard_map(local, mesh=mesh, in_specs=in_specs, out_specs=out_specs, check_vma=False)
```
